32 devices in a mesh: groups: 2 (over x), mp: 16 (over z, y, core).
Axes of the slice: x: 2, y: 2, z: 4, core: 2. Of those that a mesh axis runs over, the one named last changes fastest.
Arguments:
- tokens_in: bfloat16 [1024, 6144], P('groups', 'mp'), parts along dimension 0
- attn_gain: float32 [12288], P(('groups', 'mp')), parts along dimension 0, may hold values from 0.1 to 1.9
- w_latent: bfloat16 [12288, 512], P(('groups', 'mp')), parts along dimension 0, may hold values from -0.078125 to 0.078125
- w_query: bfloat16 [12288, 512], P(('groups', 'mp')), parts along dimension 0
- w_key_up: bfloat16 [1024, 512], P('groups', 'mp'), parts along dimension 0, may hold values from -0.25 to 0.25
- w_value_up: bfloat16 [1024, 512], P('groups', 'mp'), parts along dimension 0, may hold values from -0.25 to 0.25
- w_output: bfloat16 [1024, 6144], P('groups', 'mp'), parts along dimension 0, may hold values from -0.25 to 0.25
- ffn_gain: float32 [12288], P('groups'), parts along dimension 0, may hold values from 0.1 to 1.9
- routes: int32 [1024, 2], P('groups'), parts along dimension 0, may hold values from 0 to 3, as said below
- slots: int32 [1024, 2], P('groups'), parts along dimension 0, may hold values from 0 to 447, as said below
- gates: float32 [1024, 2], P('groups'), parts along dimension 0, may hold values from 0.2 to 1
- w_gate: bfloat16 [12288, 32768], P('groups', 'mp'), parts along dimension 0, may hold values from -0.078125 to 0.078125
- w_up: bfloat16 [12288, 32768], P('groups', 'mp'), parts along dimension 0, may hold values from -0.078125 to 0.078125
- w_down: bfloat16 [65536, 6144], P(('groups', 'mp')), parts along dimension 0, may hold values from -0.0625 to 0.0625
Outputs:
- attended: bfloat16 [1024, 6144], P('groups', 'mp'), parts along dimension 0
- expert_mix: bfloat16 [1024, 6144], P('groups', 'mp'), parts along dimension 0
The draws below stay inside these ranges and needn't reach their ends.
There are 2 independent parts, one for each index of `groups`. The reference program is written for one: setup_inputs(seed, part) draws one part's arguments, and reference() takes and returns one part's arrays. A program takes and returns all parts, laid end to end along the dimension named above; each array names one. Nothing has to cross between parts.
Inputs may be any that keep to these rules, and one draw needn't show every extreme that they name: `routes`: each token names two different experts. No expert is named by more than 448 tokens, and one expert is named by exactly 448 tokens. slots[t,k] is the slot of token t in expert routes[t,k]; the tokens that name one expert have distinct slots, from 0 up to that expert's count minus one.
All inputs are finite; a program needn't handle non-finite values.
Results may differ from the reference program's by a relative error of at most 0.0085.
The reference program's roundings to bfloat16 on the way count: a program that leaves them out, or rounds other values in their place, can miss the bound.
Values may be sent and summed in bfloat16 or wider, within the bound.
No kernel may reach another device: no remote copies, remote signals or barrier semaphores. Data moves between devices by JAX's collectives and lax.ppermute only.
A program may use at most 192 MiB of HBM per device.

```python
import jax
import jax.numpy as jnp
from jax import lax

D = 6144
HD = 128
LAT = 512
EXPERTS = 4
FF = 8192
TOKENS = 512
HEADS = 4
CAP = 448


def route_plan(key):
    key_loads, key_label, key_flip, key_order = jax.random.split(key, 4)
    remaining = 2 * TOKENS - CAP
    share = remaining // (EXPERTS - 1)
    leftover = remaining - share * (EXPERTS - 1)
    jitter = jax.random.randint(key_loads, (EXPERTS - 1,), 0, share // 4 + 1)
    others = share + jitter - jnp.roll(jitter, 1)
    others = others + leftover * (jnp.arange(EXPERTS - 1) == 0).astype(jnp.int32)
    loads = jnp.concatenate([jnp.full((1,), CAP, jnp.int32), others.astype(jnp.int32)])
    run_ends = jnp.cumsum(loads).astype(jnp.int32)
    run_starts = run_ends - loads
    position = jnp.arange(2 * TOKENS, dtype=jnp.int32)
    label = jnp.sum((position[:, None] >= run_ends[None, :]).astype(jnp.int32), axis=1).astype(jnp.int32)
    slot_of = position - run_starts[label]
    relabel = jax.random.permutation(key_label, EXPERTS).astype(jnp.int32)
    label = relabel[label]
    route_pair = jnp.stack([label[:TOKENS], label[TOKENS:]], axis=1)
    slot_pair = jnp.stack([slot_of[:TOKENS], slot_of[TOKENS:]], axis=1)
    flipped = jax.random.randint(key_flip, (TOKENS, 1), 0, 2) == 1
    route_pair = jnp.where(flipped, route_pair[:, ::-1], route_pair)
    slot_pair = jnp.where(flipped, slot_pair[:, ::-1], slot_pair)
    order = jax.random.permutation(key_order, TOKENS)
    return (route_pair[order].astype(jnp.int32), slot_pair[order].astype(jnp.int32))


def draw_routes(key, part):
    return route_plan(key)[0]


def draw_slots(key, part):
    return route_plan(key)[1]


def draw_tokens_in(key, part):
    key = jax.random.fold_in(key, 11)
    key_base = jax.random.fold_in(key, 0)
    column = jnp.arange(D, dtype=jnp.float32) / D
    base = jnp.clip(jax.random.normal(key_base, (TOKENS, D), jnp.float32), -6.0, 6.0)
    return (base * jnp.sqrt(1.0 + 2.0 * column)).astype(jnp.bfloat16)


def draw_w_query(key, part):
    key = jax.random.fold_in(key, 12)
    key_base = jax.random.fold_in(key, 0)
    base = jnp.clip(jax.random.normal(key_base, (D, HEADS * HD), jnp.float32), -6.0, 6.0)
    return (base * D ** (-0.5)).astype(jnp.bfloat16)


def level_of(own_key, shape, pieces, low, high):
    factor_of, own = 1.0, jax.random.fold_in(own_key, 6)
    for dim, shards_of in pieces:
        draws = jnp.exp(jax.random.uniform(jax.random.fold_in(own, dim), (shards_of,), jnp.float32, low / len(pieces), high / len(pieces)))
        factor_of = factor_of * jnp.repeat(draws, shape[dim] // shards_of).reshape([-1 if axis == dim else 1 for axis in range(len(shape))])
    return factor_of


def noise(key, extent, spread, reach, cuts=(), kind=jnp.bfloat16):
    gain = level_of(key, extent, cuts, -0.22, 0.18) if cuts else 1.0
    drawn = jax.random.normal(key, extent, jnp.float32) * spread * gain
    return jnp.minimum(jnp.maximum(drawn, -reach), reach).astype(kind)


def setup_inputs(seed: int = 0, part: int = 0) -> dict:
    keys = jax.random.split(jax.random.key(seed), 15)
    own_keys = jax.random.split(jax.random.fold_in(keys[14], part), 15)
    return {
        "tokens_in": draw_tokens_in(jax.random.fold_in(jax.random.fold_in(keys[14], part), 71), part),
        "attn_gain": jnp.clip(1.0 + 0.18 * jax.random.normal(own_keys[1], (D,), jnp.float32), 0.1, 1.9),
        "w_latent": noise(own_keys[2], (D, LAT), D ** -0.5, 0.078125, ((0, 16),)),
        "w_query": draw_w_query(jax.random.fold_in(jax.random.fold_in(keys[14], part), 71), part),
        "w_key_up": noise(own_keys[4], (LAT, HEADS * HD), LAT ** -0.5, 0.25, ((1, 16),)),
        "w_value_up": noise(own_keys[5], (LAT, HEADS * HD), LAT ** -0.5, 0.25, ((1, 16),)),
        "w_output": noise(own_keys[6], (HEADS * HD, D), (HEADS * HD) ** -0.5, 0.25, ((1, 16),)),
        "ffn_gain": jnp.clip(1.0 + 0.18 * jax.random.normal(own_keys[7], (D,), jnp.float32), 0.1, 1.9),
        "routes": draw_routes(jax.random.fold_in(jax.random.fold_in(keys[14], part), 71), part),
        "slots": draw_slots(jax.random.fold_in(jax.random.fold_in(keys[14], part), 71), part),
        "gates": jnp.clip(jax.random.uniform(own_keys[10], (TOKENS, 2), jnp.float32, 0.2, 1.0), 0.2, 1.0),
        "w_gate": noise(own_keys[11], (D, EXPERTS * FF), D ** -0.5, 0.078125, ((1, 16),)),
        "w_up": noise(own_keys[12], (D, EXPERTS * FF), D ** -0.5, 0.078125, ((1, 16),)),
        "w_down": noise(own_keys[13], (EXPERTS * FF, D), FF ** -0.5, 0.0625, ((0, 16),)),
    }


epsilon = 1e-05

def softmax_rows_of(scores):
    row_max = lax.optimization_barrier(jnp.max(scores, axis=1, keepdims=True))
    exp_scores = jnp.exp(scores - row_max)
    return exp_scores / lax.optimization_barrier(jnp.sum(exp_scores, axis=1, keepdims=True))

def reference(tokens_in, attn_gain, w_latent, w_query, w_key_up, w_value_up, w_output, ffn_gain, routes, slots, gates, w_gate, w_up, w_down):
    tokens_wide = tokens_in.astype(jnp.float32)
    scale_one = lax.rsqrt(lax.optimization_barrier(jnp.sum(tokens_wide * tokens_wide, axis=1)) / D + epsilon)
    normed = (tokens_wide * attn_gain.astype(jnp.float32)).astype(jnp.bfloat16)
    latent = (scale_one[:, None] * jnp.dot(normed, w_latent, preferred_element_type=jnp.float32)).astype(jnp.bfloat16)
    query_rows = (scale_one[:, None] * jnp.dot(normed, w_query, preferred_element_type=jnp.float32)).astype(jnp.bfloat16)
    positions = jnp.arange(TOKENS, dtype=jnp.int32)
    causal = positions[None, :] <= positions[:, None]

    def one_head(head_id):
        first_col = (head_id * HD).astype(jnp.int32)
        query_head = lax.dynamic_slice_in_dim(query_rows, first_col, HD, 1)
        key_map = lax.dynamic_slice_in_dim(w_key_up, first_col, HD, 1)
        value_map = lax.dynamic_slice_in_dim(w_value_up, first_col, HD, 1)
        key_rows = jnp.dot(latent, key_map, preferred_element_type=jnp.float32).astype(jnp.bfloat16)
        value_rows = jnp.dot(latent, value_map, preferred_element_type=jnp.float32).astype(jnp.bfloat16)
        scores = jnp.dot(query_head, key_rows.T, preferred_element_type=jnp.float32) * HD ** (-0.5)
        scores = jnp.where(causal, scores, -jnp.inf)
        softmax_rows = softmax_rows_of(scores).astype(jnp.bfloat16)
        return jnp.dot(softmax_rows, value_rows, preferred_element_type=jnp.float32).astype(jnp.bfloat16)
    head_outs = lax.map(one_head, jnp.arange(HEADS, dtype=jnp.int32))
    attn_sum = jnp.einsum('htk,hkd->td', head_outs.astype(jnp.float32), w_output.reshape(HEADS, HD, D).astype(jnp.float32), precision=lax.Precision.HIGHEST)
    attended = (tokens_wide + attn_sum).astype(jnp.bfloat16)
    slot_codes = (routes * CAP + slots).astype(jnp.int32)
    buffer = jnp.zeros((EXPERTS * CAP, D), jnp.bfloat16).at[slot_codes.reshape(-1)].set(jnp.repeat(attended, 2, axis=0))
    buffer_wide = buffer.astype(jnp.float32)
    scale_two = lax.rsqrt(lax.optimization_barrier(jnp.sum(buffer_wide * buffer_wide, axis=1)) / D + epsilon)
    ffn_in = (buffer_wide * scale_two[:, None] * ffn_gain.astype(jnp.float32)).astype(jnp.bfloat16)

    def one_expert(expert_id):
        row_start = (expert_id * CAP).astype(jnp.int32)
        col_start = (expert_id * FF).astype(jnp.int32)
        rows_here = lax.dynamic_slice_in_dim(ffn_in, row_start, CAP, 0)
        gate_proj = jnp.dot(rows_here, lax.dynamic_slice_in_dim(w_gate, col_start, FF, 1), preferred_element_type=jnp.float32)
        up_proj = jnp.dot(rows_here, lax.dynamic_slice_in_dim(w_up, col_start, FF, 1), preferred_element_type=jnp.float32)
        activated = (jax.nn.silu(gate_proj) * up_proj).astype(jnp.bfloat16)
        return jnp.dot(activated, lax.dynamic_slice_in_dim(w_down, col_start, FF, 0), preferred_element_type=jnp.float32)
    expert_out = lax.map(one_expert, jnp.arange(EXPERTS, dtype=jnp.int32)).reshape(EXPERTS * CAP, D)
    mixed_rows = gates[:, 0:1] * expert_out[slot_codes[:, 0]] + gates[:, 1:2] * expert_out[slot_codes[:, 1]]
    return (attended, mixed_rows.astype(jnp.bfloat16))
```

```python
import functools

import jax
import jax.numpy as jnp
from jax import lax
from jax.experimental import pallas as pl
from jax.experimental.pallas import tpu as pltpu
from jax.sharding import PartitionSpec as P

D = 6144
HD = 128
EXPERTS = 4
CAP = 448
QUAD = 4
MIB = 2**20


epsilon = 1e-05
f32 = jnp.float32
bf16 = jnp.bfloat16


def across(array, bit):
    return lax.ppermute(array, "mp", [(i, i ^ 1 << bit) for i in range(lax.axis_size("mp"))])


def across_plane(array, mask):
    return lax.ppermute(array, "mp", [(i, i ^ mask) for i in range(lax.axis_size("mp"))])


def to_plane(array, step):
    n = lax.axis_size("mp")
    return lax.ppermute(array, "mp", [(i, (i + QUAD * step) % n) for i in range(n)])


def wide_dot(a, b):
    return jnp.dot(a, b, preferred_element_type=f32)


def columns_at(array, start, width):
    return lax.dynamic_slice_in_dim(array, start, width, 1)


def rows_at(array, start, height):
    return lax.dynamic_slice_in_dim(array, start, height, 0)


def rolled_rows(array, start):
    return rows_at(jnp.concatenate([array, array], 0), start, array.shape[0])


def stage(*arrays):
    return lax.optimization_barrier(arrays)


def plane_groups(planes):
    return [[QUAD * p + q for p in range(planes)] for q in range(QUAD)]


def from_planes(array, plane, planes):
    if planes == EXPERTS:
        return [array] + [to_plane(array, -step) for step in range(1, planes)]
    every = lax.all_gather(array, "mp", axis_index_groups=plane_groups(planes))
    every = jnp.take(every, (jnp.arange(planes, dtype=jnp.int32) + plane) % planes, axis=0)
    return [every[step] for step in range(planes)]


def select_kernel(where_ref, selector_ref, scale_ref, gain_ref, a_ref, b_ref, c_ref, d_ref, out_ref):
    tokens = jnp.concatenate([a_ref[...], b_ref[...], c_ref[...], d_ref[...]], axis=0)
    rows = wide_dot(selector_ref[...], tokens)
    out_ref[...] = (rows * scale_ref[...] * gain_ref[where_ref[0]]).astype(bf16)


def select_rows(where, selector, scale, gain, pieces):
    width = pieces[0].shape[1]
    vmem = pl.BlockSpec(memory_space=pltpu.VMEM)
    return pl.pallas_call(
        select_kernel,
        in_specs=[pl.BlockSpec(memory_space=pltpu.SMEM)] + [vmem] * 7,
        out_specs=vmem,
        out_shape=jax.ShapeDtypeStruct((CAP, width), bf16),
        compiler_params=pltpu.CompilerParams(vmem_limit_bytes=16 * MIB),
        cost_estimate=pl.CostEstimate(
            flops=2 * CAP * 512 * width, bytes_accessed=2 * (512 + CAP) * width, transcendentals=0
        ),
    )(where.reshape(1), selector, scale, gain.reshape(-1, 1, width), *pieces)


def hidden_kernel(first, last, where_ref, rows_ref, gate_ref, up_ref, *refs):
    gate = wide_dot(rows_ref[...], gate_ref[...])
    up = wide_dot(rows_ref[...], up_ref[...])
    tile = gate.shape[1]
    here = pl.ds(pl.multiple_of(pl.program_id(0) * tile, tile), tile)
    if not first:
        sums_ref, _, *refs = refs
        gate = gate + sums_ref[0, :, here]
        up = up + sums_ref[1, :, here]
    out_ref, mark_ref = refs
    if not last:
        out_ref[0, :, here] = gate
        out_ref[1, :, here] = up
        mark_ref[...] = jnp.zeros_like(mark_ref)
        return
    activated = gate / (1.0 + jnp.exp(-gate)) * up
    out_ref[...] = activated.astype(bf16)
    peak = jnp.max(jnp.abs(activated).reshape(CAP // 8, 8, -1), axis=0)
    peak = jnp.max(peak, axis=1, keepdims=True)

    @pl.when(pl.program_id(0) == 0)
    def _():
        mark_ref[...] = jnp.zeros_like(mark_ref)

    mark_ref[...] = jnp.maximum(mark_ref[...], peak)


def hidden_part(where, rows, w_gate, w_up, before, last):
    width = rows.shape[1]
    units = w_gate.shape[1]
    tile = min(512, units)
    first = not before
    vmem = pl.BlockSpec(memory_space=pltpu.VMEM)
    weights = pl.BlockSpec((width, tile), lambda j, s: (s[0], j))
    if last:
        out_spec = pl.BlockSpec((CAP, tile), lambda j, s: (0, j))
        out_shape = jax.ShapeDtypeStruct((CAP, units), bf16)
    else:
        out_spec, out_shape = vmem, jax.ShapeDtypeStruct((2, CAP, units), f32)
    return pl.pallas_call(
        functools.partial(hidden_kernel, first, last),
        grid_spec=pltpu.PrefetchScalarGridSpec(
            num_scalar_prefetch=1,
            grid=(units // tile,),
            in_specs=[pl.BlockSpec((CAP, width), lambda j, s: (0, 0)), weights, weights]
            + [vmem] * len(before),
            out_specs=[out_spec, pl.BlockSpec((8, 128), lambda j, s: (0, 0))],
        ),
        out_shape=[out_shape, jax.ShapeDtypeStruct((8, 128), f32)],
        input_output_aliases={} if first or last else {4: 0},
        compiler_params=pltpu.CompilerParams(vmem_limit_bytes=40 * MIB),
        cost_estimate=pl.CostEstimate(
            flops=4 * CAP * width * units,
            bytes_accessed=4 * width * units,
            transcendentals=CAP * units,
        ),
    )(where.reshape(1), rows, w_gate, w_up, *before)


def down_kernel(blocks, marked, where_ref, act_ref, w_ref, *refs):
    product = wide_dot(act_ref[...], w_ref[...])
    half = product.shape[1] // 2
    upper = where_ref[blocks] == 1
    if marked:
        peak_ref, *refs = refs
    for index in range(blocks):

        @pl.when(pl.program_id(0) == index)
        def _():
            send_ref, keep_ref = refs[2 * index], refs[2 * index + 1]
            send_ref[:CAP] = jnp.where(upper, product[:, :half], product[:, half:])
            if marked and index == 0:
                send_ref[CAP:] = jnp.full((8, half), jnp.max(peak_ref[...]))
            keep_ref[...] = jnp.where(upper, product[:, half:], product[:, :half])


def down_parts(blocks, core, activated, w_down, width, peak=None):
    units = activated.shape[1]
    part = jax.ShapeDtypeStruct((CAP, width), f32)
    marked_part = jax.ShapeDtypeStruct((CAP + 8, width), f32)
    count = len(blocks)
    marked = peak is not None
    shapes = [part] * (2 * count)
    if marked:
        shapes[0] = marked_part
    parts = pl.pallas_call(
        functools.partial(down_kernel, count, marked),
        grid_spec=pltpu.PrefetchScalarGridSpec(
            num_scalar_prefetch=1,
            grid=(count,),
            in_specs=[
                pl.BlockSpec((CAP, units), lambda j, s: (0, 0)),
                pl.BlockSpec((units, 2 * width), lambda j, s: (0, s[j])),
            ]
            + [pl.BlockSpec((8, 128), lambda j, s: (0, 0))] * marked,
            out_specs=[pl.BlockSpec(shape.shape, lambda j, s: (0, 0)) for shape in shapes],
        ),
        out_shape=shapes,
        compiler_params=pltpu.CompilerParams(vmem_limit_bytes=40 * MIB),
        cost_estimate=pl.CostEstimate(
            flops=4 * CAP * units * width * count,
            bytes_accessed=4 * units * width * count,
            transcendentals=0,
        ),
    )(jnp.stack([*blocks, core]), activated, w_down, *([peak] if marked else []))
    return [(parts[2 * index], parts[2 * index + 1]) for index in range(count)]


def body(
    tokens_in,
    attn_gain,
    w_latent,
    w_query,
    w_key_up,
    w_value_up,
    w_output,
    ffn_gain,
    routes,
    slots,
    gates,
    w_gate,
    w_up,
    w_down,
):
    total_tokens, local_cols = tokens_in.shape
    planes = lax.axis_size("mp") // QUAD
    head_count = w_query.shape[1] // HD
    assert head_count == planes and planes % EXPERTS == 0
    latent_cols = w_latent.shape[1] // planes
    block = total_tokens // QUAD
    me = lax.axis_index("mp")
    plane, quarter = me // QUAD, me % QUAD
    side, core = quarter // 2, quarter % 2
    mine = 2 * core + side

    exact = planes == EXPERTS
    groups = plane_groups(planes)
    in_order = jnp.arange(QUAD, dtype=jnp.int32) ^ quarter
    block_order = jnp.arange(QUAD, dtype=jnp.int32) ^ mine

    tokens_wide = tokens_in.astype(f32)
    normed = (tokens_wide * attn_gain).astype(bf16)

    squares = jnp.sum(tokens_wide * tokens_wide, axis=1).reshape(1, total_tokens)

    def with_row(array, row):
        return jnp.concatenate(
            [array, jnp.pad(row, ((0, 7), (0, array.shape[1] - row.shape[1])))], axis=0
        )

    def projected(start):
        half = rows_at(normed, start * 2 * block, 2 * block)
        return jnp.concatenate([wide_dot(half, w_latent), wide_dot(half, w_query)], axis=1)

    sent = with_row(projected(1 - core), columns_at(squares, (1 - core) * 2 * block, 2 * block))
    (sent, squares) = stage(sent, squares)
    came = across(sent, 0)
    half_sum = projected(core) + came[: 2 * block]
    squares = columns_at(squares, core * 2 * block, 2 * block) + came[2 * block, : 2 * block][None]
    away = with_row(
        rows_at(half_sum, (1 - side) * block, block), columns_at(squares, (1 - side) * block, block)
    )
    stay = rows_at(half_sum, side * block, block)
    squares = columns_at(squares, side * block, block)
    away, stay, squares, tokens_in, w_key_up, w_value_up, w_output = stage(
        away, stay, squares, tokens_in, w_key_up, w_value_up, w_output
    )
    came = across(away, 1)
    plane_sum = stay + came[:block]
    squares = squares + came[block, :block][None]
    key_value_map = jnp.concatenate([w_key_up.T, w_value_up.T], axis=0)
    map_here = rolled_rows(w_output, plane * HD)
    pieces = []
    for mask in range(QUAD):
        block_there = mine ^ (2 * (mask % 2) + mask // 2)
        pieces.append(rows_at(tokens_in, block_there * block, block))
    plane_sum, squares, map_here, key_value_map, *pieces = stage(
        plane_sum, squares, map_here, key_value_map, *pieces
    )

    def share_of(target):
        return jnp.concatenate(
            [
                columns_at(plane_sum, target * latent_cols, latent_cols),
                columns_at(plane_sum, planes * latent_cols + target * HD, HD),
            ],
            axis=1,
        )

    if exact:
        sums, square_sum = share_of(plane), squares
        for step in range(1, planes):
            came = to_plane(with_row(share_of((plane + step) % planes), squares), step)
            sums = sums + came[:block]
            square_sum = square_sum + came[block, :block][None]
    else:
        square_sum = lax.psum(squares, "mp", axis_index_groups=groups)
        shares = jnp.stack([share_of(p) for p in range(planes)])
        sums = lax.all_to_all(shares, "mp", 0, 0, axis_index_groups=groups, tiled=True)
        sums = jnp.sum(sums, axis=0)
    maps = [key_value_map] + [across_plane(key_value_map, mask) for mask in range(1, QUAD)]
    scale_one = lax.rsqrt(square_sum / D + epsilon).reshape(block, 1)
    latent = (scale_one * sums[:, :latent_cols]).astype(bf16)
    query_rows = (scale_one * sums[:, latent_cols:]).astype(bf16)
    latent, query_rows, map_here, *maps = stage(latent, query_rows, map_here, *maps)

    latent = jnp.concatenate(from_planes(latent, plane, planes), axis=1)
    map_side = across(map_here, 1)
    narrow = key_value_map.shape[0] // 2
    maps = jnp.take(jnp.stack(maps), in_order, axis=0).reshape(QUAD, 2, narrow, -1)
    maps = maps.transpose(1, 0, 2, 3).reshape(2 * HD, -1).T
    maps = rolled_rows(maps, plane * latent_cols)
    latent, maps, map_here, map_side = stage(latent, maps, map_here, map_side)
    key_value = wide_dot(latent, maps).astype(bf16)
    key_value = jnp.concatenate([key_value, across(key_value, 1)], axis=0)
    columns = [map_here, across(map_here, 0), map_side, across(map_side, 0)]
    key_value, *columns = stage(key_value, *columns)
    key_value = jnp.concatenate([key_value, across(key_value, 0)], axis=0)
    scores = wide_dot(query_rows, key_value[:, :HD].T) * HD ** (-0.5)
    inside = jnp.arange(block, dtype=jnp.int32)
    key_pos = (block_order[:, None] * block + inside[None, :]).reshape(1, total_tokens)
    query_pos = (mine * block + inside)[:, None]
    scores = jnp.where(key_pos <= query_pos, scores, -jnp.inf)
    row_max = jnp.max(scores, axis=1, keepdims=True)
    exp_scores = jnp.exp(scores - row_max)
    softmax_rows = (exp_scores / jnp.sum(exp_scores, axis=1, keepdims=True)).astype(bf16)
    head_out = wide_dot(softmax_rows, key_value[:, HD:]).astype(bf16)
    head_out, routes, slots, gates, tokens_in, *columns = stage(
        head_out, routes, slots, gates, tokens_in, *columns
    )

    heads = jnp.concatenate(from_planes(head_out, plane, planes), axis=1)
    expert = plane // (planes // EXPERTS)
    slot_ids = jnp.arange(CAP, dtype=jnp.int32)
    slot_here = jnp.where(routes == expert, slots, -1)
    slot_arrived = jnp.take(slot_here.reshape(QUAD, block, 2), block_order, axis=0).reshape(-1, 2)
    chosen = (slot_arrived[:, 0][None, :] == slot_ids[:, None]) | (
        slot_arrived[:, 1][None, :] == slot_ids[:, None]
    )
    selector = chosen.astype(bf16)
    slot_gate = sum(
        jnp.sum(
            jnp.where(slot_here[:, k][None, :] == slot_ids[:, None], gates[:, k][None, :], 0.0),
            axis=1,
            keepdims=True,
        )
        for k in range(2)
    )
    output_map = jnp.take(jnp.stack(columns), in_order, axis=0)
    output_map = output_map.transpose(1, 0, 2).reshape(-1, QUAD * local_cols)
    pieces = [pieces[0]] + [across_plane(pieces[mask], mask) for mask in range(1, QUAD)]
    tokens_here = jnp.take(jnp.stack(pieces), in_order, axis=0)
    tokens_here = tokens_here.transpose(1, 0, 2).reshape(block, QUAD * local_cols)
    heads, selector, slot_gate, output_map, tokens_here = stage(
        heads, selector, slot_gate, output_map, tokens_here
    )

    attended_here = (tokens_here.astype(f32) + wide_dot(heads, output_map)).astype(bf16)
    squares = jnp.sum(jnp.square(attended_here.astype(f32)), axis=1).reshape(1, block)
    outgoing = [None] * QUAD

    def own_columns():
        for mask in range(QUAD):
            piece = columns_at(attended_here, (quarter ^ mask) * local_cols, local_cols)
            piece = piece if mask == 0 else across_plane(piece, mask)
            outgoing[2 * (mask % 2) + mask // 2] = piece
        pieces = jnp.take(jnp.stack(outgoing), block_order, axis=0)
        return pieces.reshape(total_tokens, local_cols)

    def plane_scale(square_sum):
        scale = lax.rsqrt(square_sum / D + epsilon)
        scale = [scale] + [across_plane(scale, mask) for mask in (2, 1, 3)]
        scale = jnp.concatenate(scale, axis=1)
        return jnp.sum(selector.astype(f32) * scale, axis=1, keepdims=True)

    def rows_of(span, near, far, row_scale):
        pieces = (near, far, across(near, 0), across(far, 0))
        return select_rows(span, selector, row_scale, ffn_gain, pieces)

    if not exact:
        row_scale = plane_scale(lax.psum(squares, "mp", axis_index_groups=groups))
        near = jnp.stack(from_planes(attended_here, plane, planes))
        near = jnp.take(near, (jnp.arange(planes, dtype=jnp.int32) - plane) % planes, axis=0)
        near = near.reshape(EXPERTS, planes // EXPERTS, block, QUAD * local_cols)
        near = near.transpose(0, 2, 1, 3).reshape(EXPERTS, block, -1)
        hidden = ()
        for span in range(EXPERTS):
            rows = rows_of(jnp.int32(span), near[span], across(near[span], 1), row_scale)
            last = span == EXPERTS - 1
            hidden = hidden_part(jnp.int32(span), rows, w_gate, w_up, hidden, last)
        activated = hidden[0]
        attended = own_columns()
        total = wide_dot(activated, w_down)
        incoming = lax.all_to_all(
            total.reshape(CAP, -1, local_cols), "mp", split_axis=1, concat_axis=1, tiled=True
        )
        summed = jnp.sum(incoming.reshape(CAP, EXPERTS, -1, local_cols), axis=2)
        summed = summed.reshape(CAP * EXPERTS, local_cols)
        code_row = jnp.arange(CAP * EXPERTS, dtype=jnp.int32)[None, :]
        slot_codes = slots * EXPERTS + routes
        weighting = sum(
            gates[:, k : k + 1] * (slot_codes[:, k : k + 1] == code_row).astype(f32) for k in range(2)
        )
        mixed = jnp.dot(weighting, summed, precision=lax.Precision.HIGHEST)
        return (attended, mixed.astype(bf16))

    def span(step):
        return (plane + step) % planes

    near, far = {0: attended_here}, {}
    square_sum = squares
    for step in range(1, planes):
        square_sum = square_sum + to_plane(squares, step)
    near[1] = to_plane(near[0], -1)
    far[0] = across(near[0], 1)
    row_scale = plane_scale(square_sum)
    near[0], far[0], near[1], row_scale = stage(near[0], far[0], near[1], row_scale)

    near[2] = to_plane(near[0], -2)
    far[1] = across(near[1], 1)
    rows = rows_of(span(0), near[0], far[0], row_scale)
    hidden, mark = hidden_part(span(0), rows, w_gate, w_up, (), False)
    near[0], near[1], far[1], near[2], row_scale, mark = stage(
        near[0], near[1], far[1], near[2], row_scale, mark
    )

    near[3] = to_plane(near[0], -3)
    far[2] = across(near[2], 1)
    rows = rows_of(span(1), near[1], far[1], row_scale)
    hidden, mark = hidden_part(span(1), rows, w_gate, w_up, (hidden, mark), False)
    near[2], far[2], near[3], row_scale, mark = stage(near[2], far[2], near[3], row_scale, mark)

    far[3] = across(near[3], 1)
    rows = rows_of(span(2), near[2], far[2], row_scale)
    hidden, mark = hidden_part(span(2), rows, w_gate, w_up, (hidden, mark), False)
    near[3], far[3], row_scale, mark = stage(near[3], far[3], row_scale, mark)

    rows = rows_of(span(3), near[3], far[3], row_scale)
    activated, peak = hidden_part(span(3), rows, w_gate, w_up, (hidden, mark), True)
    activated, peak, slots, routes, attended_here = stage(
        activated, peak, slots, routes, attended_here
    )

    bound = 0.0625 * QUAD * activated.shape[1] / 32768.0

    def parts_of(*wanted, peak=None):
        blocks = [2 * span(step) + (1 - side if kind == "away" else side) for kind, step in wanted]
        return down_parts(blocks, core, activated, w_down, local_cols, peak)

    def chip_sum(part):
        return part[1] + across(part[0], 0)

    def outward(total, exponent, marked):
        total = (total * jnp.exp2(-exponent)).astype(jnp.float16)
        if not marked:
            return total
        exponent = jnp.broadcast_to(exponent.astype(jnp.float16), (16, local_cols))
        return jnp.concatenate([total, exponent], axis=0)

    def exponent_of(came):
        return came[CAP, 0].astype(f32)

    def mix_of(step, result, exponent):
        source = (plane - step) % planes
        code = jnp.where(routes == source, slots, -1)
        code_row = jnp.arange(CAP, dtype=jnp.int32)[None, :]
        placing = ((code[:, 0:1] == code_row) | (code[:, 1:2] == code_row)).astype(bf16)
        result = result[:CAP].astype(f32) * jnp.exp2(exponent)
        high = result.astype(bf16)
        low = (result - high.astype(f32)).astype(bf16)
        return wide_dot(placing, high) + wide_dot(placing, low)

    (away_2,) = parts_of(("away", 2), peak=peak)
    attended = own_columns()
    activated, peak, attended, *away_2 = stage(activated, peak, attended, *away_2)

    came = across(away_2[0], 0)
    peak = jnp.maximum(jnp.max(peak), came[CAP, 0])
    exponent = jnp.ceil(jnp.log2(jnp.maximum(peak * bound, 1e-30)))
    sent_2 = outward(away_2[1] + came[:CAP], exponent, True)
    away_1, near_2 = parts_of(("away", 1), ("near", 2))
    activated, exponent, sent_2, *parts = stage(activated, exponent, sent_2, *away_1, *near_2)

    came_2 = across(sent_2, 1)
    sent_1, total_2 = outward(chip_sum(parts[:2]), exponent, False), chip_sum(parts[2:])
    away_3, away_0, near_1 = parts_of(("away", 3), ("away", 0), ("near", 1))
    activated, exponent, came_2, sent_1, total_2, *parts = stage(
        activated, exponent, came_2, sent_1, total_2, *away_3, *away_0, *near_1
    )

    there = exponent_of(came_2)
    common = jnp.maximum(exponent, there)

    def finished(total, came, marked=True):
        total = (total + came[:CAP].astype(f32) * jnp.exp2(there)) * slot_gate
        return outward(total, common, marked)

    result_2 = to_plane(finished(total_2, came_2), 2)
    came_1 = across(sent_1, 1)
    sent_3 = outward(chip_sum(parts[:2]), exponent, False)
    sent_0 = outward(chip_sum(parts[2:4]), exponent, False)
    total_1 = chip_sum(parts[4:])
    came_3 = across(sent_3, 1)
    near_3, near_0 = parts_of(("near", 3), ("near", 0))
    result_2, came_1, came_3, sent_0, total_1, there, common, *parts = stage(
        result_2, came_1, came_3, sent_0, total_1, there, common, *near_3, *near_0
    )

    result_1 = to_plane(finished(total_1, came_1), 1)
    came_0 = across(sent_0, 1)
    result_3 = to_plane(finished(chip_sum(parts[:2]), came_3), 3)
    total_0 = chip_sum(parts[2:])
    mixed = mix_of(2, result_2, exponent_of(result_2))
    result_1, result_3, total_0, came_0, there, common, mixed = stage(
        result_1, result_3, total_0, came_0, there, common, mixed
    )
    mixed = mixed + mix_of(1, result_1, exponent_of(result_1))
    mixed = mixed + mix_of(3, result_3, exponent_of(result_3))
    mixed = mixed + mix_of(0, finished(total_0, came_0, False), common)
    return (attended, mixed.astype(bf16))


def solution(mesh):
    placed = (
        P("groups", "mp"),
        P(("groups", "mp")),
        P(("groups", "mp"), None),
        P(("groups", "mp"), None),
        P("groups", "mp"),
        P("groups", "mp"),
        P("groups", "mp"),
        P("groups"),
        P("groups", None),
        P("groups", None),
        P("groups", None),
        P("groups", "mp"),
        P("groups", "mp"),
        P(("groups", "mp"), None),
    )
    return jax.shard_map(
        body,
        mesh=mesh,
        in_specs=placed,
        out_specs=(P("groups", "mp"), P("groups", "mp")),
        check_vma=False,
    )
```
